256 devices in a mesh: row: 32 (over z, x_hi, core), col: 8 (over y, x_lo).
Axes of the slice: x: 4 (x_hi: 2, x_lo: 2; x = x_hi * 2 + x_lo), y: 4, z: 8, core: 2. Of those that a mesh axis runs over, the one named last changes fastest.
Arguments:
- queries: bfloat16 [32768, 256], P(('row', 'col')), may hold values from -128 to 128
- key_states: bfloat16 [32768, 128], P(('col', 'row')), may hold values from -8 to 8
- value_states: bfloat16 [32768, 128], P(('col', 'row')), may hold values from -6 to 6
- grad_output: bfloat16 [32768, 256], P(('row', 'col')), may hold values from -6 to 6
- block_ids: int32 [16384], replicated, may hold values from 0 to 31, never falling along the last dimension, each value on 1 to 1024 neighbouring positions
Outputs:
- grad_queries: bfloat16 [32768, 256], P(('row', 'col'))
- grad_keys: bfloat16 [32768, 128], P(('col', 'row'))
- grad_values: bfloat16 [32768, 128], P(('col', 'row'))
The draws below stay inside these ranges and needn't reach their ends.
Inputs may be any that keep to these rules, and one draw needn't show every extreme that they name: `block_ids`: block numbers never fall along the clean sequence; every block from 0 to 31 holds 1 to 1024 tokens and some block holds exactly 1024. The noisy copy's token 16384 + i has the block of clean token i.
All inputs are finite; a program needn't handle non-finite values.
Results may differ from the reference program's by a relative error of at most 0.0051.
Values may be sent and summed in bfloat16 or wider, within the bound.
No kernel may reach another device: no remote copies, remote signals or barrier semaphores. Data moves between devices by JAX's collectives and lax.ppermute only.
A program may use at most 64 MiB of HBM per device.

```python
import math
import jax
import jax.numpy as jnp
import numpy as np
from jax import lax

HD = 128
HEADS = 2
BLOCK = 1024
LEN = 16384
SEQ = 32768
NBLK = 32


def base_keys(key):
    return jnp.clip(jax.random.normal(key, (SEQ, HD), jnp.float32), -6.0, 6.0)


def draw_key_states(key, part):
    keys_base = base_keys(key)
    return keys_base.astype(jnp.bfloat16)


def draw_queries(key, part):
    key = jax.random.fold_in(key, 2)
    noise = jnp.clip(jax.random.normal(key, (SEQ, HEADS * HD), jnp.float32), -6.0, 6.0)
    return noise.astype(jnp.bfloat16)


def block_levels(stream_key, extent, split, smallest, high):
    def one(axis_at, shards_of):
        steps = jax.random.uniform(jax.random.fold_in(jax.random.fold_in(stream_key, 6), axis_at), (shards_of,), jnp.float32, smallest / len(split), high / len(split))
        return jnp.repeat(jnp.exp(steps), extent[axis_at] // shards_of).reshape((-1,) + (1,) * (len(extent) - axis_at - 1))

    factor_of = one(*split[0])
    for cut in split[1:]:
        factor_of = factor_of * one(*cut)
    return factor_of


def split_up(count, total, bound, skew):
    loads = [(1 << 20) // math.isqrt(rank ** skew) + 1 for rank in range(2, count + 1)]
    surplus, counts = total - bound - (count - 1), [1] * (count - 1)
    while surplus > 0:
        movable = [i for i in range(count - 1) if counts[i] < bound]
        mass, budget = sum([loads[i] for i in movable]), surplus
        for i in movable:
            addition = min(bound - counts[i], max(1, budget * loads[i] // mass), surplus)
            counts[i] = counts[i] + addition
            surplus = surplus - addition
    return np.array([bound] + counts)


def uneven(key, amount, total, reach, slope):
    if amount == 2:
        one = jax.random.randint(key, (), max(1, total - reach), min(reach, total - 1) + 1)
        return jnp.stack([one, total - one])
    sizes = jnp.asarray(split_up(amount, total, reach, slope), jnp.int32)
    couples = (amount - 1) // 2
    giver, sink = sizes[1:1 + 2 * couples:2], sizes[2:2 + 2 * couples:2]
    margin = jnp.minimum(giver - 1, reach - sink)
    moved = jax.random.randint(jax.random.fold_in(key, 1), (couples,), 0, 1 << 20) % (margin + 1)
    sizes = sizes.at[1:1 + 2 * couples:2].set(giver - moved).at[2:2 + 2 * couples:2].set(sink + moved)
    return sizes[jax.random.permutation(jax.random.fold_in(key, 2), amount)]


def centred(stream_key, extent, deviation, bound, split=(), kind=jnp.bfloat16):
    drawn = deviation * jax.random.normal(stream_key, extent, jnp.float32)
    if split:
        drawn = drawn * block_levels(stream_key, extent, split, -0.22, 0.18)
    return jnp.clip(drawn, -bound, bound).astype(kind)


def setup_inputs(seed: int = 0) -> dict:
    splits = jax.random.split(jax.random.key(seed), 6)
    return {
        "queries": draw_queries(jax.random.fold_in(splits[5], 71), 0),
        "key_states": draw_key_states(jax.random.fold_in(splits[5], 71), 0),
        "value_states": centred(splits[2], (SEQ, HD), 1.0, 6.0, ((0, 256),)),
        "grad_output": centred(splits[3], (SEQ, HEADS * HD), 1.0, 6.0, ((0, 256),)),
        "block_ids": jnp.searchsorted(jnp.cumsum(uneven(splits[4], NBLK, LEN, BLOCK, 0)), jnp.arange(LEN), side="right").astype(jnp.int32),
    }


def allowed(query_block, query_noisy, key_block, key_noisy):
    clean_key = jnp.logical_not(key_noisy)
    earlier = key_block < query_block
    same_block = key_block == query_block
    from_clean = clean_key & (earlier | same_block & jnp.logical_not(query_noisy))
    from_noisy = key_noisy & query_noisy & same_block
    return from_clean | from_noisy

def reference(queries, key_states, value_states, grad_output, block_ids):
    seq_total = queries.shape[0]
    head_dim = key_states.shape[1]
    head_count = queries.shape[1] // head_dim
    score_scale = 1.0 / math.sqrt(head_dim)
    positions = jnp.arange(seq_total, dtype=jnp.int32)
    block_all = jnp.concatenate([block_ids, block_ids]).astype(jnp.int32)
    noisy_all = positions >= block_ids.shape[0]
    block_rows = math.gcd(seq_total, 512)
    block_count = seq_total // block_rows
    keys_wide = key_states.astype(jnp.float32)
    values_wide = value_states.astype(jnp.float32)

    def visit(running, inputs):
        grad_key_sum, grad_value_sum = running
        query_rows, grad_rows, query_block, query_noisy = inputs
        query_heads = query_rows.astype(jnp.float32).reshape(block_rows, head_count, head_dim)
        grad_heads = grad_rows.astype(jnp.float32).reshape(block_rows, head_count, head_dim)
        scores = jnp.einsum('ihd,jd->ihj', query_heads, keys_wide) * score_scale
        visible = allowed(query_block[:, None, None], query_noisy[:, None, None], block_all[None, None, :], noisy_all[None, None, :])
        row_max = lax.optimization_barrier(jnp.max(jnp.where(visible, scores, -jnp.inf), axis=2, keepdims=True))
        weights = jnp.where(visible, jnp.exp(scores - row_max), 0.0)
        attn_probs = weights / lax.optimization_barrier(jnp.sum(weights, axis=2, keepdims=True))
        grad_probs = jnp.einsum('ihd,jd->ihj', grad_heads, values_wide)
        row_delta = lax.optimization_barrier(jnp.sum(attn_probs * grad_probs, axis=2, keepdims=True))
        grad_scores = attn_probs * (grad_probs - row_delta)
        probs_low = lax.optimization_barrier(attn_probs.astype(jnp.bfloat16)).astype(jnp.float32)
        scaled_low = lax.optimization_barrier((grad_scores * score_scale).astype(jnp.bfloat16)).astype(jnp.float32)
        grad_query = jnp.einsum('ihj,jd->ihd', scaled_low, keys_wide).reshape(block_rows, head_count * head_dim)
        grad_key_sum = grad_key_sum + jnp.einsum('ihj,ihd->jd', scaled_low, query_heads)
        grad_value_sum = grad_value_sum + jnp.einsum('ihj,ihd->jd', probs_low, grad_heads)
        return ((grad_key_sum, grad_value_sum), grad_query.astype(jnp.bfloat16))
    empty_grads = jnp.zeros((seq_total, head_dim), jnp.float32)
    inputs = (queries.reshape(block_count, block_rows, -1), grad_output.reshape(block_count, block_rows, -1), block_all.reshape(block_count, block_rows), noisy_all.reshape(block_count, block_rows))
    (grad_key_sum, grad_value_sum), grad_query = lax.scan(visit, (empty_grads, empty_grads), inputs)
    return (grad_query.reshape(seq_total, -1), grad_key_sum.astype(jnp.bfloat16), grad_value_sum.astype(jnp.bfloat16))
```

```python
import functools
import math

import jax
import jax.numpy as jnp
from jax import lax
from jax.experimental import pallas as pl
from jax.experimental.pallas import tpu as pltpu
from jax.sharding import Mesh
from jax.sharding import PartitionSpec as P

bf16 = jnp.bfloat16
f32 = jnp.float32
i32 = jnp.int32
NZ, NXH, NCORE, NY, NXL = 8, 2, 2, 4, 2
NX = NXH * NXL
CH = 128
HD = 128
RUN = NXH * NCORE * CH
NRUN = NY * NXL
HALF = NRUN // 2
LOW = -1e30
SCALE = 1.0 / math.sqrt(HD)
LOG2E = math.log2(math.e)
ROWS = ("z", "xh", "core")
COLS = ("y", "xl")
XAX = ("xh", "xl")


def shift(x, axis, size, by):
    return lax.ppermute(x, axis, [(i, (i + by) % size) for i in range(size)])


def nt(a, b):
    return lax.dot_general(a, b, (((1,), (1,)), ((), ())), preferred_element_type=f32)


def nn(a, b):
    return lax.dot_general(a, b, (((1,), (0,)), ((), ())), preferred_element_type=f32)


def load_all(ids, q_pieces, k_own, k_other, qs, kvs, sem):
    z, y, xh, xl, core = ids[0], ids[1], ids[2], ids[3], ids[4]
    copies = []
    for r, by in enumerate(Q_SHIFTS):
        copies.append((q_pieces[r], qs.at[(z - by) % NZ]))
    x = xh * NXL + xl
    for s in range(NY):
        for k in range(NX):
            px = (x - k) % NX
            py = (y - s) % NY
            slot = py * NXL + px % NXL
            for refs, pc in ((k_own, core), (k_other, 1 - core)):
                at = pl.multiple_of((px // NXL) * (NCORE * CH) + pc * CH, CH)
                copies.append((refs[s].at[k], kvs.at[slot, pl.ds(at, CH)]))
    copies = [pltpu.make_async_copy(a, b, sem.at[n]) for n, (a, b) in enumerate(copies)]
    for c in copies:
        c.start()
    for c in copies:
        c.wait()


Q_SHIFTS = (0, 1, -1, 2, -2, 3, -3, 4)
N_COPIES = NZ + NCORE * NY * NX


def key_columns(kid_ref, kcol):
    for b in range(HALF):
        row = kid_ref[b : b + 1, :]
        kcol[b] = jnp.broadcast_to(row, (CH, RUN)).T


def both_heads(qo, base):
    return jnp.concatenate([qo[:, base : base + HD], qo[:, base + HD : base + 2 * HD]], axis=0)


def mask_of(kcol_b, qrow, noisy_q, noisy_k):
    if noisy_k:
        seen = kcol_b == qrow
    else:
        seen = kcol_b <= jnp.where(noisy_q, qrow - 1, qrow)
    return jnp.concatenate([seen, seen], axis=1)


def for_live(mm, body):
    def clean(n, carry):
        j = n // HALF
        b = n % HALF
        a = j % HALF
        less = jnp.where(j >= HALF, 1, 0)
        live = mm[2, b] <= mm[1, a] - less
        full = mm[3, b] <= mm[0, a] - less

        @pl.when(live & full)
        def _():
            body(j, b, b, a, False, False)

        @pl.when(live & jnp.logical_not(full))
        def _():
            body(j, b, b, a, True, False)

        return carry

    def noisy(n, carry):
        a = n // HALF
        b = n % HALF
        live = (mm[2, b] <= mm[1, a]) & (mm[3, b] >= mm[0, a])

        @pl.when(live)
        def _():
            body(a + HALF, b + HALF, b, a, True, True)

        return carry

    lax.fori_loop(0, NZ * HALF, clean, 0)
    lax.fori_loop(0, HALF * HALF, noisy, 0)


def stats_kernel(ids, mm, qid_ref, kid_ref, *refs):
    q_pieces, k_own, k_other = refs[:NZ], refs[NZ : NZ + NY], refs[NZ + NY : NZ + 2 * NY]
    out_ref = refs[NZ + 2 * NY]
    qs, kvs, kcol, top, total, dot, sem = refs[NZ + 2 * NY + 1 :]
    load_all(ids, q_pieces, k_own, k_other, qs, kvs, sem)
    key_columns(kid_ref, kcol)
    top[...] = jnp.full(top.shape, LOW, f32)
    total[...] = jnp.zeros(total.shape, f32)
    dot[...] = jnp.zeros(dot.shape, f32)
    c = SCALE * LOG2E

    def body(j, slot, b, a, masked, noisy_k):
        qo = qs[j]
        kv = kvs[slot]
        s = nt(kv[:, :HD], both_heads(qo, 0)) * c
        dp = nt(kv[:, HD:], both_heads(qo, 2 * HD))
        if masked:
            seen = mask_of(kcol[b], qid_ref[pl.ds(a, 1)][0], j >= HALF, noisy_k)
            s = jnp.where(seen, s, LOW)
        old = top[j]
        new = jnp.maximum(old, jnp.max(s, axis=0, keepdims=True))
        p = jnp.exp2(s - new)
        if masked:
            p = jnp.where(seen, p, 0.0)
        f = jnp.exp2(old - new)
        top[j] = new
        total[j] = total[j] * f + jnp.sum(p, axis=0, keepdims=True)
        dot[j] = dot[j] * f + jnp.sum(p * dp, axis=0, keepdims=True)

    for_live(mm, body)
    t = total[...]
    some = t > 0.0
    safe = jnp.where(some, t, 1.0)
    out_ref[:, 0:1, :] = jnp.where(some, top[...] + jnp.log2(safe), LOW)
    out_ref[:, 1:2, :] = jnp.where(some, dot[...] / safe, 0.0)


def grad_kernel(ids, mm, qid_ref, kid_ref, st_ref, *refs):
    q_pieces, k_own, k_other = refs[:NZ], refs[NZ : NZ + NY], refs[NZ + NY : NZ + 2 * NY]
    dq_ref, own_ref, other_ref = refs[NZ + 2 * NY : NZ + 2 * NY + 3]
    qs, kvs, kcol, kts, lse, delta, dq_acc, dkv_acc, sem = refs[NZ + 2 * NY + 3 :]
    load_all(ids, q_pieces, k_own, k_other, qs, kvs, sem)
    key_columns(kid_ref, kcol)
    for b in range(NRUN):
        kts[b] = kvs[b][:, :HD].T
    parts = st_ref[:, :, 0:1, :]
    high = jnp.max(parts, axis=0)
    shares = jnp.exp2(parts - high[None])
    sums = jnp.sum(shares, axis=0)
    lse[...] = high + jnp.log2(sums)
    delta[...] = jnp.sum(shares * st_ref[:, :, 1:2, :], axis=0) / sums
    dq_acc[...] = jnp.zeros(dq_acc.shape, f32)
    dkv_acc[...] = jnp.zeros(dkv_acc.shape, f32)
    c = SCALE * LOG2E

    def body(j, slot, b, a, masked, noisy_k):
        qo = qs[j]
        kv = kvs[slot]
        q2 = both_heads(qo, 0)
        o2 = both_heads(qo, 2 * HD)
        s = nt(kv[:, :HD], q2) * c
        dp = nt(kv[:, HD:], o2)
        p = jnp.exp2(s - lse[j])
        if masked:
            seen = mask_of(kcol[b], qid_ref[pl.ds(a, 1)][0], j >= HALF, noisy_k)
            p = jnp.where(seen, p, 0.0)
        ds = (p * (dp - delta[j]) * SCALE).astype(bf16)
        dkv_acc[slot, :, :HD] += nn(ds, q2)
        dkv_acc[slot, :, HD:] += nn(p.astype(bf16), o2)
        dq_acc[j] += nn(kts[slot], ds)

    for_live(mm, body)
    for j in range(NZ):
        t = dq_acc[j]
        dq_ref[j] = jnp.concatenate([t[:, :CH].T, t[:, CH:].T], axis=1).astype(bf16)
    core = ids[4]
    for slot in range(NRUN):
        for xh in range(NXH):
            y, x = slot // NXL, xh * NXL + slot % NXL
            at = xh * NCORE * CH
            own_at = pl.multiple_of(at + core * CH, CH)
            other_at = pl.multiple_of(at + (1 - core) * CH, CH)
            own_ref[y * NX + x] = dkv_acc[slot, pl.ds(own_at, CH), :].astype(bf16)
            other_ref[y * NX + x] = dkv_acc[slot, pl.ds(other_at, CH), :].astype(bf16)


SMEM = pl.BlockSpec(memory_space=pltpu.SMEM)
VMEM = pl.BlockSpec(memory_space=pltpu.VMEM)
ANY = pl.BlockSpec(memory_space=pl.ANY)
BIG = 48 << 20
LOADS = [
    pltpu.VMEM((NZ, CH, 4 * HD), bf16),
    pltpu.VMEM((NRUN, RUN, 2 * HD), bf16),
    pltpu.VMEM((HALF, RUN, CH), i32),
]
ROW = pltpu.VMEM((NZ, 1, 2 * CH), f32)
SEMS = pltpu.SemaphoreType.DMA((N_COPIES,))


def per_device(queries, key_states, value_states, grad_output, block_ids):
    z, xh, core = (lax.axis_index(n) for n in ROWS)
    y, xl = (lax.axis_index(n) for n in COLS)
    qo = jnp.concatenate([queries, grad_output], axis=1)
    kv = jnp.concatenate([key_states, value_states], axis=1)

    def swap(t):
        return lax.ppermute(t, "core", [(0, 1), (1, 0)])

    xs = jnp.stack([kv] + [shift(kv, XAX, NX, k) for k in range(1, NX)])
    k_own = [xs] + [shift(xs, "y", NY, s) for s in range(1, NY)]
    k_other = [swap(t) for t in k_own]
    pieces = {0: qo}
    for s in range(1, NZ // 2 + 1):
        pieces[s] = shift(pieces[s - 1], "z", NZ, 1)
        if s < NZ // 2:
            pieces[-s] = shift(pieces[1 - s], "z", NZ, -1)
    q_pieces = [pieces[s] for s in Q_SHIFTS]

    qid = block_ids.reshape(HALF, NXH * NCORE * NY * NXL, CH)
    place = ((xh * NCORE + core) * NY + y) * NXL + xl
    qid = lax.dynamic_slice_in_dim(qid, place, 1, 1)
    kid = block_ids.reshape(HALF, NZ, RUN)
    kid = lax.dynamic_slice_in_dim(kid, z, 1, 1).reshape(HALF, RUN)
    mm = jnp.stack([qid[:, 0, 0], qid[:, 0, CH - 1], kid[:, 0], kid[:, RUN - 1]])
    ids = jnp.stack([z, y, xh, xl, core]).astype(i32)
    data = (*q_pieces, *k_own, *k_other)

    stats = pl.pallas_call(
        stats_kernel,
        out_shape=jax.ShapeDtypeStruct((NZ, 2, 2 * CH), f32),
        in_specs=[SMEM, SMEM, VMEM, VMEM] + [ANY] * len(data),
        out_specs=VMEM,
        scratch_shapes=LOADS + [ROW, ROW, ROW, SEMS],
        compiler_params=pltpu.CompilerParams(vmem_limit_bytes=BIG),
    )(ids, mm, qid, kid, *data)
    stats = jnp.broadcast_to(stats[None], (NZ,) + stats.shape)
    stats = lax.all_to_all(stats, "z", 0, 0)
    dq, own, other = pl.pallas_call(
        grad_kernel,
        out_shape=(
            jax.ShapeDtypeStruct((NZ, CH, 2 * HD), bf16),
            jax.ShapeDtypeStruct((NY * NX, CH, 2 * HD), bf16),
            jax.ShapeDtypeStruct((NY * NX, CH, 2 * HD), bf16),
        ),
        in_specs=[SMEM, SMEM, VMEM, VMEM, VMEM] + [ANY] * len(data),
        out_specs=(VMEM, VMEM, VMEM),
        scratch_shapes=LOADS
        + [
            pltpu.VMEM((NRUN, HD, RUN), bf16),
            ROW,
            ROW,
            pltpu.VMEM((NZ, HD, 2 * CH), f32),
            pltpu.VMEM((NRUN, RUN, 2 * HD), f32),
            SEMS,
        ],
        compiler_params=pltpu.CompilerParams(vmem_limit_bytes=BIG),
    )(ids, mm, qid, kid, stats, *data)
    pair = (own.astype(f32) + swap(other).astype(f32)).astype(bf16)
    pair = lax.all_to_all(pair, ("y", "xh", "xl"), 0, 0)
    dq = lax.all_to_all(dq, "z", 0, 0)
    pair = jnp.sum(pair.astype(f32), axis=0).astype(bf16)
    dq = jnp.sum(dq.astype(f32), axis=0).astype(bf16)
    return dq, pair[:, :HD], pair[:, HD:]


def solution(mesh):
    fine = Mesh(mesh.devices.reshape(NZ, NXH, NCORE, NY, NXL), ROWS + COLS)
    by_row = P(ROWS + COLS, None)
    by_col = P(COLS + ROWS, None)
    return jax.shard_map(
        per_device,
        mesh=fine,
        in_specs=(by_row, by_col, by_col, by_row, P()),
        out_specs=(by_row, by_col, by_col),
        check_vma=False,
    )
```

```python
import functools
import math

import jax
import jax.numpy as jnp
from jax import lax
from jax.experimental import pallas as pl
from jax.experimental.pallas import tpu as pltpu
from jax.sharding import Mesh
from jax.sharding import PartitionSpec as P

bf16 = jnp.bfloat16
f32 = jnp.float32
i32 = jnp.int32
NZ, NXH, NCORE, NY, NXL = 8, 2, 2, 4, 2
NX = NXH * NXL
CH = 128
HD = 128
RUN = NXH * NCORE * CH
NRUN = NY * NXL
HALF = NRUN // 2
NBLK = 32
LOW = -1e30
SCALE = 1.0 / math.sqrt(HD)
FACTOR = SCALE * math.log2(math.e)
ROWS = ("z", "xh", "core")
COLS = ("y", "xl")
XAX = ("xh", "xl")


def shift(x, axis, size, by):
    return lax.ppermute(x, axis, [(i, (i + by) % size) for i in range(size)])


def nt(a, b):
    return lax.dot_general(a, b, (((1,), (1,)), ((), ())), preferred_element_type=f32)


def nn(a, b):
    return lax.dot_general(a, b, (((1,), (0,)), ((), ())), preferred_element_type=f32)


def load_all(ids, q_pieces, k_own, k_other, qs, kvs, sem):
    z, y, xh, xl, core = ids[0], ids[1], ids[2], ids[3], ids[4]
    copies = []
    for r, by in enumerate(Q_SHIFTS):
        copies.append((q_pieces[r], qs.at[(z - by) % NZ]))
    x = xh * NXL + xl
    for s in range(NY):
        for k in range(NX):
            px = (x - k) % NX
            py = (y - s) % NY
            slot = py * NXL + px % NXL
            for refs, pc in ((k_own, core), (k_other, 1 - core)):
                at = pl.multiple_of((px // NXL) * (NCORE * CH) + pc * CH, CH)
                copies.append((refs[s].at[k], kvs.at[slot, pl.ds(at, CH)]))
    copies = [pltpu.make_async_copy(a, b, sem.at[n]) for n, (a, b) in enumerate(copies)]
    for c in copies:
        c.start()
    return copies


Q_SHIFTS = (0, 1, -1, 2, -2, 3, -3, 4)
N_COPIES = NZ + NCORE * NY * NX


def masks(qid_ref, kid_ref, hot, bias):
    lane = lax.broadcasted_iota(i32, (RUN, CH), 1)
    for b in range(HALF):
        col = jnp.broadcast_to(kid_ref[b : b + 1, :], (CH, RUN)).T
        hot[b] = jnp.where(lane == col, 1.0, 0.0).astype(bf16)
        hot[b + HALF] = jnp.where(lane == col + NBLK, 1.0, 0.0).astype(bf16)
    lane = lax.broadcasted_iota(i32, (CH, CH), 1)
    for a in range(HALF):
        col = jnp.broadcast_to(qid_ref[a], (CH, CH)).T
        bias[a] = jnp.where(lane <= col, 0.0, LOW).astype(bf16)
        seen = (lane < col) | (lane == col + NBLK)
        bias[a + HALF] = jnp.where(seen, 0.0, LOW).astype(bf16)


def both_heads(qo, base):
    return jnp.concatenate([qo[:, base : base + HD], qo[:, base + HD : base + 2 * HD]], axis=0)


def scores(k, q2, hot, bias):
    return nt(
        jnp.concatenate([k, hot], axis=1),
        jnp.concatenate([q2, jnp.concatenate([bias, bias], axis=0)], axis=1),
    )


def for_live(mm, body):
    def visit(n, carry):
        a = n // HALF
        b = n % HALF

        @pl.when(mm[2, b] <= mm[1, a])
        def _():
            body((a, a + HALF), b)

        @pl.when((mm[2, b] <= mm[1, a]) & (mm[3, b] >= mm[0, a]))
        def _():
            body((a + HALF,), b + HALF)

        return carry

    lax.fori_loop(0, HALF * HALF, visit, 0)


def stats_kernel(ids, mm, qid_ref, kid_ref, *refs):
    q_pieces, k_own, k_other = refs[:NZ], refs[NZ : NZ + NY], refs[NZ + NY : NZ + 2 * NY]
    out_ref = refs[NZ + 2 * NY]
    qs, kvs, hot, bias, top, total, dot, sem = refs[NZ + 2 * NY + 1 :]
    copies = load_all(ids, q_pieces, k_own, k_other, qs, kvs, sem)
    masks(qid_ref, kid_ref, hot, bias)
    for c in copies:
        c.wait()
    top[...] = jnp.full(top.shape, LOW, f32)
    total[...] = jnp.zeros(total.shape, f32)
    dot[...] = jnp.zeros(dot.shape, f32)

    def body(chunks, slot):
        ss = [scores(kvs[slot, :, :HD], both_heads(qs[j], 0), hot[slot], bias[j]) for j in chunks]
        dps = [nt(kvs[slot, :, HD:], both_heads(qs[j], 2 * HD)) for j in chunks]
        for j, s, dp in zip(chunks, ss, dps):
            old = top[j]
            new = jnp.maximum(old, jnp.max(s, axis=0, keepdims=True))
            p = jnp.exp2((s - new) * FACTOR)
            f = jnp.exp2((old - new) * FACTOR)
            top[j] = new
            total[j] = total[j] * f + jnp.sum(p, axis=0, keepdims=True)
            dot[j] = dot[j] * f + jnp.sum(p * dp, axis=0, keepdims=True)

    for_live(mm, body)
    t = total[...]
    some = t > 0.0
    safe = jnp.where(some, t, 1.0)
    out_ref[:, 0:1, :] = jnp.where(some, top[...] * FACTOR + jnp.log2(safe), LOW)
    out_ref[:, 1:2, :] = dot[...] / safe


def grad_kernel(ids, mm, qid_ref, kid_ref, st_ref, *refs):
    q_pieces, k_own, k_other = refs[:NZ], refs[NZ : NZ + NY], refs[NZ + NY : NZ + 2 * NY]
    dq_ref, own_ref, other_ref = refs[NZ + 2 * NY : NZ + 2 * NY + 3]
    qs, kvs, hot, bias, kts, lse, delta, dq_acc, dkv_acc, sem = refs[NZ + 2 * NY + 3 :]
    copies = load_all(ids, q_pieces, k_own, k_other, qs, kvs, sem)
    masks(qid_ref, kid_ref, hot, bias)
    parts = st_ref[:, :, 0:1, :]
    high = jnp.max(parts, axis=0)
    shares = jnp.exp2(parts - high[None])
    sums = jnp.sum(shares, axis=0)
    lse[...] = high + jnp.log2(sums)
    delta[...] = jnp.sum(shares * st_ref[:, :, 1:2, :], axis=0) / sums
    dq_acc[...] = jnp.zeros(dq_acc.shape, f32)
    dkv_acc[...] = jnp.zeros(dkv_acc.shape, f32)
    for c in copies:
        c.wait()

    def body(chunks, slot):
        q2s, o2s, dss, ps = [], [], [], []
        for j in chunks:
            qo = qs[j]
            q2 = both_heads(qo, 0)
            o2 = both_heads(qo, 2 * HD)
            s = scores(kvs[slot, :, :HD], q2, hot[slot], bias[j])
            dp = nt(kvs[slot, :, HD:], o2)
            p = jnp.exp2(s * FACTOR - lse[j])
            ds = (p * (dp - delta[j]) * SCALE).astype(bf16)
            q2s.append(q2)
            o2s.append(o2)
            dss.append(ds)
            ps.append(p.astype(bf16))
        q2, o2 = jnp.concatenate(q2s, axis=0), jnp.concatenate(o2s, axis=0)
        ds, p = jnp.concatenate(dss, axis=1), jnp.concatenate(ps, axis=1)
        dq = lax.dot_general(ds, kvs[slot, :, :HD], (((0,), (0,)), ((), ())), preferred_element_type=f32)
        for i, j in enumerate(chunks):
            dq_acc[j] += dq[2 * CH * i : 2 * CH * (i + 1)]
        dkv_acc[slot, :, :HD] += nn(ds, q2)
        dkv_acc[slot, :, HD:] += nn(p, o2)

    for_live(mm, body)
    for j in range(NZ):
        t = dq_acc[j]
        dq_ref[j] = jnp.concatenate([t[:CH], t[CH:]], axis=1).astype(bf16)
    core = ids[4]
    for slot in range(NRUN):
        for xh in range(NXH):
            y, x = slot // NXL, xh * NXL + slot % NXL
            at = xh * NCORE * CH
            own_at = pl.multiple_of(at + core * CH, CH)
            other_at = pl.multiple_of(at + (1 - core) * CH, CH)
            own_ref[y, x] = dkv_acc[slot, pl.ds(own_at, CH), :].astype(bf16)
            other_ref[y, x] = dkv_acc[slot, pl.ds(other_at, CH), :].astype(bf16)


SMEM = pl.BlockSpec(memory_space=pltpu.SMEM)
VMEM = pl.BlockSpec(memory_space=pltpu.VMEM)
ANY = pl.BlockSpec(memory_space=pl.ANY)
BIG = 60 << 20
LOADS = [
    pltpu.VMEM((NZ, CH, 4 * HD), bf16),
    pltpu.VMEM((NRUN, RUN, 2 * HD), bf16),
    pltpu.VMEM((NRUN, RUN, CH), bf16),
    pltpu.VMEM((NZ, CH, CH), bf16),
]
ROW = pltpu.VMEM((NZ, 1, 2 * CH), f32)
SEMS = pltpu.SemaphoreType.DMA((N_COPIES,))


def per_device(queries, key_states, value_states, grad_output, block_ids):
    z, xh, core = (lax.axis_index(n) for n in ROWS)
    y, xl = (lax.axis_index(n) for n in COLS)
    qo = jnp.concatenate([queries, grad_output], axis=1)
    kv = jnp.concatenate([key_states, value_states], axis=1)

    def swap(t):
        return lax.ppermute(t, "core", [(0, 1), (1, 0)])

    xs = jnp.stack([kv] + [shift(kv, XAX, NX, k) for k in range(1, NX)])
    k_own = [xs] + [shift(xs, "y", NY, s) for s in range(1, NY)]
    k_other = [swap(t) for t in k_own]
    pieces = {0: qo}
    for s in range(1, NZ // 2 + 1):
        pieces[s] = shift(pieces[s - 1], "z", NZ, 1)
        if s < NZ // 2:
            pieces[-s] = shift(pieces[1 - s], "z", NZ, -1)
    q_pieces = [pieces[s] for s in Q_SHIFTS]

    qid = block_ids.reshape(HALF, NXH * NCORE * NY * NXL, CH)
    place = ((xh * NCORE + core) * NY + y) * NXL + xl
    qid = lax.dynamic_slice_in_dim(qid, place, 1, 1)
    kid = block_ids.reshape(HALF, NZ, RUN)
    kid = lax.dynamic_slice_in_dim(kid, z, 1, 1).reshape(HALF, RUN)
    mm = jnp.stack([qid[:, 0, 0], qid[:, 0, CH - 1], kid[:, 0], kid[:, RUN - 1]])
    ids = jnp.stack([z, y, xh, xl, core]).astype(i32)
    data = (*q_pieces, *k_own, *k_other)

    stats = stats_call(ids, mm, qid, kid, data)
    stats = jnp.broadcast_to(stats[None], (NZ,) + stats.shape)
    stats = lax.all_to_all(stats, "z", 0, 0)
    dq, own, other = grad_call(ids, mm, qid, kid, stats, data)

    dq = lax.all_to_all(dq, "z", 0, 0)
    pair = (own.astype(f32) + swap(other).astype(f32)).astype(bf16)
    pair = scatter(pair, y, "y", NY)
    pair = scatter(pair, xh * NXL + xl, XAX, NX)
    dq = jnp.sum(dq.astype(f32), axis=0).astype(bf16)
    return dq, pair[:, :HD], pair[:, HD:]


def scatter(t, me, axis, size):
    def part(k):
        return lax.dynamic_index_in_dim(t, (me + k) % size, 0, keepdims=False)

    got = [part(0)] + [shift(part(k), axis, size, k) for k in range(1, size)]
    return sum(g.astype(f32) for g in got).astype(bf16)


def stats_call(ids, mm, qid, kid, data):
    return pl.pallas_call(
        stats_kernel,
        out_shape=jax.ShapeDtypeStruct((NZ, 2, 2 * CH), f32),
        in_specs=[SMEM, SMEM, VMEM, VMEM] + [ANY] * len(data),
        out_specs=VMEM,
        scratch_shapes=LOADS + [ROW, ROW, ROW, SEMS],
        compiler_params=pltpu.CompilerParams(vmem_limit_bytes=BIG),
    )(ids, mm, qid, kid, *data)


def grad_call(ids, mm, qid, kid, stats, data):
    return pl.pallas_call(
        grad_kernel,
        out_shape=(
            jax.ShapeDtypeStruct((NZ, CH, 2 * HD), bf16),
            jax.ShapeDtypeStruct((NY, NX, CH, 2 * HD), bf16),
            jax.ShapeDtypeStruct((NY, NX, CH, 2 * HD), bf16),
        ),
        in_specs=[SMEM, SMEM, VMEM, VMEM, VMEM] + [ANY] * len(data),
        out_specs=(VMEM, VMEM, VMEM),
        scratch_shapes=LOADS
        + [
            pltpu.VMEM((NRUN, HD, RUN), bf16),
            ROW,
            ROW,
            pltpu.VMEM((NZ, 2 * CH, HD), f32),
            pltpu.VMEM((NRUN, RUN, 2 * HD), f32),
            SEMS,
        ],
        compiler_params=pltpu.CompilerParams(vmem_limit_bytes=BIG),
    )(ids, mm, qid, kid, stats, *data)


def solution(mesh):
    fine = Mesh(mesh.devices.reshape(NZ, NXH, NCORE, NY, NXL), ROWS + COLS)
    by_row = P(ROWS + COLS, None)
    by_col = P(COLS + ROWS, None)
    return jax.shard_map(
        per_device,
        mesh=fine,
        in_specs=(by_row, by_col, by_col, by_row, P()),
        out_specs=(by_row, by_col, by_col),
        check_vma=False,
    )
```

```python
import functools
import math

import jax
import jax.numpy as jnp
from jax import lax
from jax.experimental import pallas as pl
from jax.experimental.pallas import tpu as pltpu
from jax.sharding import Mesh
from jax.sharding import PartitionSpec as P

bf16 = jnp.bfloat16
f32 = jnp.float32
i32 = jnp.int32
NZ, NXH, NCORE, NY, NXL = 8, 2, 2, 4, 2
NX = NXH * NXL
CH = 128
HD = 128
RUN = NXH * NCORE * CH
NRUN = NY * NXL
HALF = NRUN // 2
NBLK = 32
LOW = -1e30
SCALE = 1.0 / math.sqrt(HD)
FACTOR = SCALE * math.log2(math.e)
ROWS = ("z", "xh", "core")
COLS = ("y", "xl")
XAX = ("xh", "xl")


def shift(x, axis, size, by):
    return lax.ppermute(x, axis, [(i, (i + by) % size) for i in range(size)])


def nt(a, b):
    return lax.dot_general(a, b, (((1,), (1,)), ((), ())), preferred_element_type=f32)


def nn(a, b):
    return lax.dot_general(a, b, (((1,), (0,)), ((), ())), preferred_element_type=f32)


def load_all(ids, q_pieces, k_own, k_other, qs, kvs, sem):
    z, core = ids[0], ids[4]
    copies = []
    for r, by in enumerate(Q_SHIFTS):
        copies.append((q_pieces[r], qs.at[(z - by) % NZ]))
    for y in range(NY):
        for xh in range(NXH):
            for ref, pc in ((k_own, core), (k_other, 1 - core)):
                at = pl.multiple_of(xh * (NCORE * CH) + pc * CH, CH)
                copies.append(
                    (
                        ref.at[pl.ds(y * NX + xh * NXL, NXL)],
                        kvs.at[pl.ds(y * NXL, NXL), pl.ds(at, CH)],
                    )
                )
    copies = [pltpu.make_async_copy(a, b, sem.at[n]) for n, (a, b) in enumerate(copies)]
    for c in copies:
        c.start()
    return copies


Q_SHIFTS = (0, 1, -1, 2, -2, 3, -3, 4)
N_COPIES = NZ + NCORE * NY * NXH


def pack_kernel(q_ref, o_ref, k_ref, v_ref, qo_ref, kv_ref):
    qo_ref[:, : 2 * HD] = q_ref[...]
    qo_ref[:, 2 * HD :] = o_ref[...]
    for i in range(NY * NX):
        kv_ref[i, :, :HD] = k_ref[...]
        kv_ref[i, :, HD:] = v_ref[...]


def masks(qid_ref, kid_ref, hot, bias):
    lane = lax.broadcasted_iota(i32, (RUN, CH), 1)
    for b in range(HALF):
        col = jnp.broadcast_to(kid_ref[b : b + 1, :], (CH, RUN)).T
        hot[b] = jnp.where(lane == col, 1.0, 0.0).astype(bf16)
        hot[b + HALF] = jnp.where(lane == col + NBLK, 1.0, 0.0).astype(bf16)
    lane = lax.broadcasted_iota(i32, (CH, CH), 1)
    for a in range(HALF):
        col = jnp.broadcast_to(qid_ref[a], (CH, CH)).T
        bias[a] = jnp.where(lane <= col, 0.0, LOW).astype(bf16)
        seen = (lane < col) | (lane == col + NBLK)
        bias[a + HALF] = jnp.where(seen, 0.0, LOW).astype(bf16)


def both_heads(qo, base):
    return jnp.concatenate([qo[:, base : base + HD], qo[:, base + HD : base + 2 * HD]], axis=0)


def scores(k, q2, hot, bias):
    return nt(
        jnp.concatenate([k, hot], axis=1),
        jnp.concatenate([q2, jnp.concatenate([bias, bias], axis=0)], axis=1),
    )


def for_rest(mm, body):
    def visit(n, carry):
        a = n // HALF
        b = n % HALF

        @pl.when((b > a) & (mm[2, b] <= mm[1, a]))
        def _():
            body((a,), b)

        @pl.when((mm[2, b] <= mm[1, a]) & (mm[3, b] >= mm[0, a]))
        def _():
            body((a + HALF,), b + HALF)

        return carry

    lax.fori_loop(0, HALF * HALF, visit, 0)


def stats_kernel(ids, mm, qid_ref, kid_ref, *refs):
    q_pieces, k_own, k_other = refs[:NZ], refs[NZ], refs[NZ + 1]
    out_ref, qs, kvs, hot, bias, top, total, dot, sem = refs[NZ + 2 :]
    copies = load_all(ids, q_pieces, k_own, k_other, qs, kvs, sem)
    masks(qid_ref, kid_ref, hot, bias)
    for c in copies:
        c.wait()
    top[...] = jnp.full(top.shape, LOW, f32)
    total[...] = jnp.zeros(total.shape, f32)
    dot[...] = jnp.zeros(dot.shape, f32)

    def update(j, s, dp):
        old = top[j]
        new = jnp.maximum(old, jnp.max(s, axis=0, keepdims=True))
        p = jnp.exp2((s - new) * FACTOR)
        f = jnp.exp2((old - new) * FACTOR)
        top[j] = new
        total[j] = total[j] * f + jnp.sum(p, axis=0, keepdims=True)
        dot[j] = dot[j] * f + jnp.sum(p * dp, axis=0, keepdims=True)

    def body(chunks, slot):
        ss = [scores(kvs[slot, :, :HD], both_heads(qs[j], 0), hot[slot], bias[j]) for j in chunks]
        dps = [nt(kvs[slot, :, HD:], both_heads(qs[j], 2 * HD)) for j in chunks]
        for j, s, dp in zip(chunks, ss, dps):
            update(j, s, dp)

    for a in range(HALF):
        keys = kvs[: a + 1].reshape((a + 1) * RUN, 2 * HD)
        blocks = hot[: a + 1].reshape((a + 1) * RUN, CH)
        js = (a, a + HALF)
        ss = [scores(keys[:, :HD], both_heads(qs[j], 0), blocks, bias[j]) for j in js]
        dps = [nt(keys[:, HD:], both_heads(qs[j], 2 * HD)) for j in js]
        for j, s, dp in zip(js, ss, dps):
            update(j, s, dp)

    for_rest(mm, body)
    t = total[...]
    some = t > 0.0
    safe = jnp.where(some, t, 1.0)
    out_ref[:, 0:1, :] = jnp.where(some, top[...] * FACTOR + jnp.log2(safe), LOW)
    out_ref[:, 1:2, :] = dot[...] / safe


def grad_kernel(
    ids,
    mm,
    st_ref,
    qs,
    kvs,
    hot,
    bias,
    dq_ref,
    own_ref,
    other_ref,
    lse,
    delta,
    dq_acc,
    dkv_acc,
):
    parts = st_ref[:, :, 0:1, :]
    high = jnp.max(parts, axis=0)
    shares = jnp.exp2(parts - high[None])
    sums = jnp.sum(shares, axis=0)
    lse[...] = high + jnp.log2(sums)
    delta[...] = jnp.sum(shares * st_ref[:, :, 1:2, :], axis=0) / sums
    dkv_acc[HALF:] = jnp.zeros((HALF, RUN, 2 * HD), f32)

    def visit(js, keys, blocks):
        q2s = [both_heads(qs[j], 0) for j in js]
        o2s = [both_heads(qs[j], 2 * HD) for j in js]
        ss = [scores(keys[:, :HD], q2, blocks, bias[j]) for j, q2 in zip(js, q2s)]
        dps = [nt(keys[:, HD:], o2) for o2 in o2s]
        ps = [jnp.exp2(s * FACTOR - lse[j]) for j, s in zip(js, ss)]
        dss = [
            (p * (dp - delta[j]) * SCALE).astype(bf16) for j, p, dp in zip(js, ps, dps)
        ]
        q2, o2 = jnp.concatenate(q2s, axis=0), jnp.concatenate(o2s, axis=0)
        ds = jnp.concatenate(dss, axis=1)
        p = jnp.concatenate([p.astype(bf16) for p in ps], axis=1)
        dq = lax.dot_general(
            ds, keys[:, :HD], (((0,), (0,)), ((), ())), preferred_element_type=f32
        )
        return dq, nn(ds, q2), nn(p, o2)

    def body(chunks, slot):
        dq, dk, dv = visit(chunks, kvs[slot], hot[slot])
        for i, j in enumerate(chunks):
            dq_acc[j] += dq[2 * CH * i : 2 * CH * (i + 1)]
        dkv_acc[slot, :, :HD] += dk
        dkv_acc[slot, :, HD:] += dv

    for a in reversed(range(HALF)):
        runs = a + 1
        keys = kvs[:runs].reshape(runs * RUN, 2 * HD)
        blocks = hot[:runs].reshape(runs * RUN, CH)
        dq, dk, dv = visit((a, a + HALF), keys, blocks)
        dq_acc[a] = dq[: 2 * CH]
        dq_acc[a + HALF] = dq[2 * CH :]
        dk, dv = dk.reshape(runs, RUN, HD), dv.reshape(runs, RUN, HD)
        if runs == HALF:
            dkv_acc[:runs, :, :HD] = dk
            dkv_acc[:runs, :, HD:] = dv
        else:
            dkv_acc[:runs, :, :HD] += dk
            dkv_acc[:runs, :, HD:] += dv

    for_rest(mm, body)
    for j in range(NZ):
        t = dq_acc[j]
        dq_ref[j] = jnp.concatenate([t[:CH], t[CH:]], axis=1).astype(bf16)
    core = ids[4]
    for slot in range(NRUN):
        for xh in range(NXH):
            y, x = slot // NXL, xh * NXL + slot % NXL
            at = xh * NCORE * CH
            own_at = pl.multiple_of(at + core * CH, CH)
            other_at = pl.multiple_of(at + (1 - core) * CH, CH)
            own_ref[y, x] = dkv_acc[slot, pl.ds(own_at, CH), :].astype(bf16)
            other_ref[y, x] = dkv_acc[slot, pl.ds(other_at, CH), :].astype(bf16)


SMEM = pl.BlockSpec(memory_space=pltpu.SMEM)
VMEM = pl.BlockSpec(memory_space=pltpu.VMEM)
ANY = pl.BlockSpec(memory_space=pl.ANY)
DATA = VMEM
BIG = 44 << 20
LOADS = (
    jax.ShapeDtypeStruct((NZ, CH, 4 * HD), bf16),
    jax.ShapeDtypeStruct((NRUN, RUN, 2 * HD), bf16),
    jax.ShapeDtypeStruct((NRUN, RUN, CH), bf16),
    jax.ShapeDtypeStruct((NZ, CH, CH), bf16),
)
ROW = pltpu.VMEM((NZ, 1, 2 * CH), f32)
SEMS = pltpu.SemaphoreType.DMA((N_COPIES,))


def per_device(queries, key_states, value_states, grad_output, block_ids):
    z, xh, core = (lax.axis_index(n) for n in ROWS)
    y, xl = (lax.axis_index(n) for n in COLS)
    qo, kv = pl.pallas_call(
        pack_kernel,
        out_shape=(
            jax.ShapeDtypeStruct((CH, 4 * HD), bf16),
            jax.ShapeDtypeStruct((NY * NX, CH, 2 * HD), bf16),
        ),
        in_specs=[VMEM] * 4,
        out_specs=(VMEM, VMEM),
    )(queries, grad_output, key_states, value_states)

    def swap(t):
        return lax.ppermute(t, "core", [(0, 1), (1, 0)])

    k_own = lax.all_to_all(kv, ("y",) + XAX, 0, 0)
    pieces = {0: qo}
    for s in range(1, NZ // 2 + 1):
        pieces[s] = shift(pieces[s - 1], "z", NZ, 1)
        if s < NZ // 2:
            pieces[-s] = shift(pieces[1 - s], "z", NZ, -1)
    q_pieces = [pieces[s] for s in Q_SHIFTS]
    k_late, _, _ = lax.optimization_barrier((k_own, pieces[-3], pieces[3]))
    k_other = swap(k_late)

    qid = block_ids.reshape(HALF, NXH * NCORE * NY * NXL, CH)
    place = ((xh * NCORE + core) * NY + y) * NXL + xl
    qid = lax.dynamic_slice_in_dim(qid, place, 1, 1)
    kid = block_ids.reshape(HALF, NZ, RUN)
    kid = lax.dynamic_slice_in_dim(kid, z, 1, 1).reshape(HALF, RUN)
    mm = jnp.stack([qid[:, 0, 0], qid[:, 0, CH - 1], kid[:, 0], kid[:, RUN - 1]])
    ids = jnp.stack([z, y, xh, xl, core]).astype(i32)
    data = (*q_pieces, k_own, k_other)

    stats, *held = stats_call(ids, mm, qid, kid, data)
    stats = jnp.broadcast_to(stats[None], (NZ,) + stats.shape)
    stats = lax.all_to_all(stats, "z", 0, 0)
    dq, own, other = grad_call(ids, mm, stats, held)

    dq = lax.all_to_all(dq, "z", 0, 0)
    pair = (own.astype(f32) + swap(other).astype(f32)).astype(bf16)
    pair = scatter(pair, y, "y", NY)
    pair = scatter(pair, xh * NXL + xl, XAX, NX)
    dq = jnp.sum(dq.astype(f32), axis=0).astype(bf16)
    return dq, pair[:, :HD], pair[:, HD:]


def scatter(t, me, axis, size):
    def part(k):
        return lax.dynamic_index_in_dim(t, (me + k) % size, 0, keepdims=False)

    got = [part(0)] + [shift(part(k), axis, size, k) for k in range(1, size)]
    return sum(g.astype(f32) for g in got).astype(bf16)


def stats_call(ids, mm, qid, kid, data):
    return pl.pallas_call(
        stats_kernel,
        out_shape=(jax.ShapeDtypeStruct((NZ, 2, 2 * CH), f32),) + LOADS,
        in_specs=[SMEM, SMEM, VMEM, VMEM] + [DATA] * len(data),
        out_specs=(VMEM,) * 5,
        scratch_shapes=[ROW, ROW, ROW, SEMS],
        compiler_params=pltpu.CompilerParams(vmem_limit_bytes=BIG),
    )(ids, mm, qid, kid, *data)


def grad_call(ids, mm, stats, held):
    return pl.pallas_call(
        grad_kernel,
        out_shape=(
            jax.ShapeDtypeStruct((NZ, CH, 2 * HD), bf16),
            jax.ShapeDtypeStruct((NY, NX, CH, 2 * HD), bf16),
            jax.ShapeDtypeStruct((NY, NX, CH, 2 * HD), bf16),
        ),
        in_specs=[SMEM, SMEM] + [VMEM] * 5,
        out_specs=(VMEM, VMEM, VMEM),
        scratch_shapes=[
            ROW,
            ROW,
            pltpu.VMEM((NZ, 2 * CH, HD), f32),
            pltpu.VMEM((NRUN, RUN, 2 * HD), f32),
        ],
        compiler_params=pltpu.CompilerParams(vmem_limit_bytes=BIG),
    )(ids, mm, stats, *held)


def solution(mesh):
    fine = Mesh(mesh.devices.reshape(NZ, NXH, NCORE, NY, NXL), ROWS + COLS)
    by_row = P(ROWS + COLS, None)
    by_col = P(COLS + ROWS, None)
    return jax.shard_map(
        per_device,
        mesh=fine,
        in_specs=(by_row, by_col, by_col, by_row, P()),
        out_specs=(by_row, by_col, by_col),
        check_vma=False,
    )
```

```python
import functools
import math

import jax
import jax.numpy as jnp
from jax import lax
from jax.experimental import pallas as pl
from jax.experimental.pallas import tpu as pltpu
from jax.sharding import Mesh
from jax.sharding import PartitionSpec as P

bf16 = jnp.bfloat16
f32 = jnp.float32
i32 = jnp.int32
NZ, NXH, NCORE, NY, NXL = 8, 2, 2, 4, 2
NX = NXH * NXL
CH = 128
HD = 128
RUN = NXH * NCORE * CH
NRUN = NY * NXL
HALF = NRUN // 2
NBLK = 32
LOW = -1e30
SCALE = 1.0 / math.sqrt(HD)
FACTOR = SCALE * math.log2(math.e)
ROWS = ("z", "xh", "core")
COLS = ("y", "xl")
XAX = ("xh", "xl")


def shift(x, axis, size, by):
    return lax.ppermute(x, axis, [(i, (i + by) % size) for i in range(size)])


def nt(a, b):
    return lax.dot_general(a, b, (((1,), (1,)), ((), ())), preferred_element_type=f32)


def nn(a, b):
    return lax.dot_general(a, b, (((1,), (0,)), ((), ())), preferred_element_type=f32)


def load_all(ids, q_pieces, k_own, k_other, qs, kvs, sem):
    z, core = ids[0], ids[4]
    copies = []
    for r, by in enumerate(Q_SHIFTS):
        copies.append((q_pieces[r], qs.at[(z - by) % NZ]))
    for y in range(NY):
        for xh in range(NXH):
            for ref, pc in ((k_own, core), (k_other, 1 - core)):
                at = pl.multiple_of(xh * (NCORE * CH) + pc * CH, CH)
                copies.append(
                    (
                        ref.at[pl.ds(y * NX + xh * NXL, NXL)],
                        kvs.at[pl.ds(y * NXL, NXL), pl.ds(at, CH)],
                    )
                )
    copies = [pltpu.make_async_copy(a, b, sem.at[n]) for n, (a, b) in enumerate(copies)]
    for c in copies:
        c.start()
    return copies


Q_SHIFTS = (0, 1, -1, 2, -2, 3, -3, 4)
N_COPIES = NZ + NCORE * NY * NXH


def pack_kernel(q_ref, o_ref, k_ref, v_ref, qo_ref, kv_ref):
    qo_ref[:, : 2 * HD] = q_ref[...]
    qo_ref[:, 2 * HD :] = o_ref[...]
    for i in range(NY * NX):
        kv_ref[i, :, :HD] = k_ref[...]
        kv_ref[i, :, HD:] = v_ref[...]


def masks(qid_ref, kid_ref, hot, bias):
    lane = lax.broadcasted_iota(i32, (RUN, CH), 1)
    for b in range(HALF):
        col = jnp.broadcast_to(kid_ref[b : b + 1, :], (CH, RUN)).T
        hot[b] = jnp.where(lane == col, 1.0, 0.0).astype(bf16)
        hot[b + HALF] = jnp.where(lane == col + NBLK, 1.0, 0.0).astype(bf16)
    lane = lax.broadcasted_iota(i32, (CH, CH), 1)
    for a in range(HALF):
        col = jnp.broadcast_to(qid_ref[a], (CH, CH)).T
        bias[a] = jnp.where(lane <= col, 0.0, LOW).astype(bf16)
        seen = (lane < col) | (lane == col + NBLK)
        bias[a + HALF] = jnp.where(seen, 0.0, LOW).astype(bf16)


def both_heads(qo, base):
    return jnp.concatenate([qo[:, base : base + HD], qo[:, base + HD : base + 2 * HD]], axis=0)


def scores(k, q2, hot, bias):
    return nt(
        jnp.concatenate([k, hot], axis=1),
        jnp.concatenate([q2, jnp.concatenate([bias, bias], axis=0)], axis=1),
    )


def for_rest(mm, body):
    def shared(a, b):
        return (mm[2, b] <= mm[1, a]) & (mm[3, b] >= mm[0, a])

    def any_of(flags):
        return functools.reduce(jnp.logical_or, flags)

    steps = range(HALF - 1)

    @pl.when(any_of([shared(a, a) for a in range(HALF)]))
    def _():
        body([(a + HALF, a + HALF) for a in range(HALF)])

    @pl.when(any_of([shared(a, a + 1) for a in steps]))
    def _():
        body([(a, a + 1) for a in steps] + [(a + HALF, a + HALF + 1) for a in steps])

    @pl.when(any_of([shared(a + 1, a) for a in steps]))
    def _():
        body([(a + HALF + 1, a + HALF) for a in steps])


def stats_kernel(ids, mm, qid_ref, kid_ref, *refs):
    q_pieces, k_own, k_other = refs[:NZ], refs[NZ], refs[NZ + 1]
    out_ref, qs, kvs, hot, bias, top, total, dot, sem = refs[NZ + 2 :]
    copies = load_all(ids, q_pieces, k_own, k_other, qs, kvs, sem)
    masks(qid_ref, kid_ref, hot, bias)
    for c in copies:
        c.wait()
    top[...] = jnp.full(top.shape, LOW, f32)
    total[...] = jnp.zeros(total.shape, f32)
    dot[...] = jnp.zeros(dot.shape, f32)

    def update(j, s, dp):
        old = top[j]
        new = jnp.maximum(old, jnp.max(s, axis=0, keepdims=True))
        p = jnp.exp2((s - new) * FACTOR)
        f = jnp.exp2((old - new) * FACTOR)
        top[j] = new
        total[j] = total[j] * f + jnp.sum(p, axis=0, keepdims=True)
        dot[j] = dot[j] * f + jnp.sum(p * dp, axis=0, keepdims=True)

    def body(pairs):
        ss = [scores(kvs[b, :, :HD], both_heads(qs[j], 0), hot[b], bias[j]) for j, b in pairs]
        dps = [nt(kvs[b, :, HD:], both_heads(qs[j], 2 * HD)) for j, b in pairs]
        for (j, _), s, dp in zip(pairs, ss, dps):
            update(j, s, dp)

    for a in range(HALF):
        keys = kvs[: a + 1].reshape((a + 1) * RUN, 2 * HD)
        blocks = hot[: a + 1].reshape((a + 1) * RUN, CH)
        js = (a, a + HALF)
        ss = [scores(keys[:, :HD], both_heads(qs[j], 0), blocks, bias[j]) for j in js]
        dps = [nt(keys[:, HD:], both_heads(qs[j], 2 * HD)) for j in js]
        for j, s, dp in zip(js, ss, dps):
            update(j, s, dp)

    for_rest(mm, body)
    t = total[...]
    some = t > 0.0
    safe = jnp.where(some, t, 1.0)
    out_ref[:, 0:1, :] = jnp.where(some, top[...] * FACTOR + jnp.log2(safe), LOW)
    out_ref[:, 1:2, :] = dot[...] / safe


def grad_kernel(
    ids,
    mm,
    st_ref,
    qs,
    kvs,
    hot,
    bias,
    dq_ref,
    own_ref,
    other_ref,
    lse,
    delta,
    dq_acc,
    dkv_acc,
):
    parts = st_ref[:, :, 0:1, :]
    high = jnp.max(parts, axis=0)
    shares = jnp.exp2(parts - high[None])
    sums = jnp.sum(shares, axis=0)
    lse[...] = high + jnp.log2(sums)
    delta[...] = jnp.sum(shares * st_ref[:, :, 1:2, :], axis=0) / sums
    dkv_acc[HALF:] = jnp.zeros((HALF, RUN, 2 * HD), f32)

    def start(j, keys, blocks):
        q2 = both_heads(qs[j], 0)
        o2 = both_heads(qs[j], 2 * HD)
        s = scores(keys[:, :HD], q2, blocks, bias[j])
        dp = nt(keys[:, HD:], o2)
        p = jnp.exp2(s * FACTOR - lse[j])
        ds = (p * (dp - delta[j]) * SCALE).astype(bf16)
        return q2, o2, ds, p.astype(bf16)

    def query_grad(ds, keys):
        return lax.dot_general(
            ds, keys[:, :HD], (((0,), (0,)), ((), ())), preferred_element_type=f32
        )

    def visit(js, keys, blocks):
        parts = [start(j, keys, blocks) for j in js]
        q2, o2 = (jnp.concatenate([t[n] for t in parts], axis=0) for n in (0, 1))
        ds, p = (jnp.concatenate([t[n] for t in parts], axis=1) for n in (2, 3))
        return query_grad(ds, keys), nn(ds, q2), nn(p, o2)

    def body(pairs):
        parts = [start(j, kvs[b], hot[b]) for j, b in pairs]
        for (j, b), (q2, o2, ds, p) in zip(pairs, parts):
            dq_acc[j] += query_grad(ds, kvs[b])
            dkv_acc[b, :, :HD] += nn(ds, q2)
            dkv_acc[b, :, HD:] += nn(p, o2)

    for a in reversed(range(HALF)):
        runs = a + 1
        keys = kvs[:runs].reshape(runs * RUN, 2 * HD)
        blocks = hot[:runs].reshape(runs * RUN, CH)
        dq, dk, dv = visit((a, a + HALF), keys, blocks)
        dq_acc[a] = dq[: 2 * CH]
        dq_acc[a + HALF] = dq[2 * CH :]
        dk, dv = dk.reshape(runs, RUN, HD), dv.reshape(runs, RUN, HD)
        if runs == HALF:
            dkv_acc[:runs, :, :HD] = dk
            dkv_acc[:runs, :, HD:] = dv
        else:
            dkv_acc[:runs, :, :HD] += dk
            dkv_acc[:runs, :, HD:] += dv

    for_rest(mm, body)
    for j in range(NZ):
        t = dq_acc[j]
        dq_ref[j] = jnp.concatenate([t[:CH], t[CH:]], axis=1).astype(bf16)
    core = ids[4]
    for slot in range(NRUN):
        for xh in range(NXH):
            y, x = slot // NXL, xh * NXL + slot % NXL
            at = xh * NCORE * CH
            own_at = pl.multiple_of(at + core * CH, CH)
            other_at = pl.multiple_of(at + (1 - core) * CH, CH)
            own_ref[y, x] = dkv_acc[slot, pl.ds(own_at, CH), :].astype(bf16)
            other_ref[y, x] = dkv_acc[slot, pl.ds(other_at, CH), :].astype(bf16)


SMEM = pl.BlockSpec(memory_space=pltpu.SMEM)
VMEM = pl.BlockSpec(memory_space=pltpu.VMEM)
ANY = pl.BlockSpec(memory_space=pl.ANY)
DATA = VMEM
BIG = 44 << 20
LOADS = (
    jax.ShapeDtypeStruct((NZ, CH, 4 * HD), bf16),
    jax.ShapeDtypeStruct((NRUN, RUN, 2 * HD), bf16),
    jax.ShapeDtypeStruct((NRUN, RUN, CH), bf16),
    jax.ShapeDtypeStruct((NZ, CH, CH), bf16),
)
ROW = pltpu.VMEM((NZ, 1, 2 * CH), f32)
SEMS = pltpu.SemaphoreType.DMA((N_COPIES,))


def per_device(queries, key_states, value_states, grad_output, block_ids):
    z, xh, core = (lax.axis_index(n) for n in ROWS)
    y, xl = (lax.axis_index(n) for n in COLS)
    qo, kv = pl.pallas_call(
        pack_kernel,
        out_shape=(
            jax.ShapeDtypeStruct((CH, 4 * HD), bf16),
            jax.ShapeDtypeStruct((NY * NX, CH, 2 * HD), bf16),
        ),
        in_specs=[VMEM] * 4,
        out_specs=(VMEM, VMEM),
    )(queries, grad_output, key_states, value_states)

    def swap(t):
        return lax.ppermute(t, "core", [(0, 1), (1, 0)])

    k_own = lax.all_to_all(kv, ("y",) + XAX, 0, 0)
    pieces = {0: qo}
    for s in range(1, NZ // 2 + 1):
        pieces[s] = shift(pieces[s - 1], "z", NZ, 1)
        if s < NZ // 2:
            pieces[-s] = shift(pieces[1 - s], "z", NZ, -1)
    q_pieces = [pieces[s] for s in Q_SHIFTS]
    k_late, _, _ = lax.optimization_barrier((k_own, pieces[-3], pieces[3]))
    k_other = swap(k_late)

    qid = block_ids.reshape(HALF, NXH * NCORE * NY * NXL, CH)
    place = ((xh * NCORE + core) * NY + y) * NXL + xl
    qid = lax.dynamic_slice_in_dim(qid, place, 1, 1)
    kid = block_ids.reshape(HALF, NZ, RUN)
    kid = lax.dynamic_slice_in_dim(kid, z, 1, 1).reshape(HALF, RUN)
    mm = jnp.stack([qid[:, 0, 0], qid[:, 0, CH - 1], kid[:, 0], kid[:, RUN - 1]])
    ids = jnp.stack([z, y, xh, xl, core]).astype(i32)
    data = (*q_pieces, k_own, k_other)

    stats, *held = stats_call(ids, mm, qid, kid, data)
    stats = jnp.broadcast_to(stats[None], (NZ,) + stats.shape)
    stats = lax.all_to_all(stats, "z", 0, 0)
    dq, own, other = grad_call(ids, mm, stats, held)

    dq = lax.all_to_all(dq, "z", 0, 0)
    pair = (own.astype(f32) + swap(other).astype(f32)).astype(bf16)
    pair = scatter(pair, y, "y", NY)
    pair = scatter(pair, xh * NXL + xl, XAX, NX)
    dq = jnp.sum(dq.astype(f32), axis=0).astype(bf16)
    return dq, pair[:, :HD], pair[:, HD:]


def scatter(t, me, axis, size):
    def part(k):
        return lax.dynamic_index_in_dim(t, (me + k) % size, 0, keepdims=False)

    got = [part(0)] + [shift(part(k), axis, size, k) for k in range(1, size)]
    return sum(g.astype(f32) for g in got).astype(bf16)


def stats_call(ids, mm, qid, kid, data):
    return pl.pallas_call(
        stats_kernel,
        out_shape=(jax.ShapeDtypeStruct((NZ, 2, 2 * CH), f32),) + LOADS,
        in_specs=[SMEM, SMEM, VMEM, VMEM] + [DATA] * len(data),
        out_specs=(VMEM,) * 5,
        scratch_shapes=[ROW, ROW, ROW, SEMS],
        compiler_params=pltpu.CompilerParams(vmem_limit_bytes=BIG),
    )(ids, mm, qid, kid, *data)


def grad_call(ids, mm, stats, held):
    return pl.pallas_call(
        grad_kernel,
        out_shape=(
            jax.ShapeDtypeStruct((NZ, CH, 2 * HD), bf16),
            jax.ShapeDtypeStruct((NY, NX, CH, 2 * HD), bf16),
            jax.ShapeDtypeStruct((NY, NX, CH, 2 * HD), bf16),
        ),
        in_specs=[SMEM, SMEM] + [VMEM] * 5,
        out_specs=(VMEM, VMEM, VMEM),
        scratch_shapes=[
            ROW,
            ROW,
            pltpu.VMEM((NZ, 2 * CH, HD), f32),
            pltpu.VMEM((NRUN, RUN, 2 * HD), f32),
        ],
        compiler_params=pltpu.CompilerParams(vmem_limit_bytes=BIG),
    )(ids, mm, stats, *held)


def solution(mesh):
    fine = Mesh(mesh.devices.reshape(NZ, NXH, NCORE, NY, NXL), ROWS + COLS)
    by_row = P(ROWS + COLS, None)
    by_col = P(COLS + ROWS, None)
    return jax.shard_map(
        per_device,
        mesh=fine,
        in_specs=(by_row, by_col, by_col, by_row, P()),
        out_specs=(by_row, by_col, by_col),
        check_vma=False,
    )
```

```python
import functools
import math

import jax
import jax.numpy as jnp
from jax import lax
from jax.experimental import pallas as pl
from jax.experimental.pallas import tpu as pltpu
from jax.sharding import Mesh
from jax.sharding import PartitionSpec as P

bf16 = jnp.bfloat16
f32 = jnp.float32
i32 = jnp.int32
NZ, NXH, NCORE, NY, NXL = 8, 2, 2, 4, 2
NX = NXH * NXL
CH = 128
HD = 128
RUN = NXH * NCORE * CH
NRUN = NY * NXL
HALF = NRUN // 2
NBLK = 32
LOW = -1e30
SCALE = 1.0 / math.sqrt(HD)
FACTOR = SCALE * math.log2(math.e)
ROWS = ("z", "xh", "core")
COLS = ("y", "xl")
XAX = ("xh", "xl")


def shift(x, axis, size, by):
    return lax.ppermute(x, axis, [(i, (i + by) % size) for i in range(size)])


def nt(a, b):
    return lax.dot_general(a, b, (((1,), (1,)), ((), ())), preferred_element_type=f32)


def nn(a, b):
    return lax.dot_general(a, b, (((1,), (0,)), ((), ())), preferred_element_type=f32)


def load_queries(ids, q_pieces, qs):
    for by, piece in zip(Q_SHIFTS, q_pieces):
        qs[(ids[0] - by) % NZ] = piece[...]


def run_of(own_ref, other_ref, slot):
    at = slot // NXL * NX + slot % NXL
    return [ref[at + xh * NXL] for ref in (own_ref, other_ref) for xh in range(NXH)]


def runs_of(own_ref, other_ref, slots):
    return jnp.concatenate([t for n in slots for t in run_of(own_ref, other_ref, n)], axis=0)


Q_SHIFTS = (0, 1, -1, 2, -2, 3, -3, 4)


def pack_kernel(q_ref, o_ref, k_ref, v_ref, qo_ref, kv_ref):
    qo_ref[:, : 2 * HD] = q_ref[...]
    qo_ref[:, 2 * HD :] = o_ref[...]
    for i in range(NY * NX):
        kv_ref[i, :, :HD] = k_ref[...]
        kv_ref[i, :, HD:] = v_ref[...]


def make_masks(qid_ref, kid_ref, hot, bias):
    lane = lax.broadcasted_iota(i32, (RUN, CH), 1)
    for b in range(HALF):
        col = jnp.broadcast_to(kid_ref[b : b + 1, :], (CH, RUN)).T
        hot[b] = jnp.where(lane == col, 1.0, 0.0).astype(bf16)
        hot[b + HALF] = jnp.where(lane == col + NBLK, 1.0, 0.0).astype(bf16)
    lane = lax.broadcasted_iota(i32, (CH, CH), 1)
    for a in range(HALF):
        col = jnp.broadcast_to(qid_ref[a], (CH, CH)).T
        bias[a] = jnp.where(lane <= col, 0.0, LOW).astype(bf16)
        seen = (lane < col) | (lane == col + NBLK)
        bias[a + HALF] = jnp.where(seen, 0.0, LOW).astype(bf16)


def both_heads(qo, base):
    return jnp.concatenate([qo[:, base : base + HD], qo[:, base + HD : base + 2 * HD]], axis=0)


def scores(k, q2, hot, bias):
    return nt(
        jnp.concatenate([k, hot], axis=1),
        jnp.concatenate([q2, jnp.concatenate([bias, bias], axis=0)], axis=1),
    )


def for_rest(mm, body):
    def shared(a, b):
        return (mm[2, b] <= mm[1, a]) & (mm[3, b] >= mm[0, a])

    def any_of(flags):
        return functools.reduce(jnp.logical_or, flags)

    steps = range(HALF - 1)

    @pl.when(any_of([shared(a, a) for a in range(HALF)]))
    def _():
        body([(a + HALF, a + HALF) for a in range(HALF)])

    @pl.when(any_of([shared(a, a + 1) for a in steps]))
    def _():
        body([(a, a + 1) for a in steps] + [(a + HALF, a + HALF + 1) for a in steps])

    @pl.when(any_of([shared(a + 1, a) for a in steps]))
    def _():
        body([(a + HALF + 1, a + HALF) for a in steps])


def stats_kernel(ids, mm, qid_ref, kid_ref, k_own, k_other, *refs):
    q_pieces, (out_ref, qs, hot, bias, top, total, dot) = refs[:NZ], refs[NZ:]
    load_queries(ids, q_pieces, qs)
    make_masks(qid_ref, kid_ref, hot, bias)
    top[...] = jnp.full(top.shape, LOW, f32)
    total[...] = jnp.zeros(total.shape, f32)
    dot[...] = jnp.zeros(dot.shape, f32)

    def update(j, s, dp):
        old = top[j]
        new = jnp.maximum(old, jnp.max(s, axis=0, keepdims=True))
        p = jnp.exp2((s - new) * FACTOR)
        f = jnp.exp2((old - new) * FACTOR)
        top[j] = new
        total[j] = total[j] * f + jnp.sum(p, axis=0, keepdims=True)
        dot[j] = dot[j] * f + jnp.sum(p * dp, axis=0, keepdims=True)

    def body(pairs):
        ss, dps = [], []
        for j, b in pairs:
            keys = runs_of(k_own, k_other, [b])
            ss.append(scores(keys[:, :HD], both_heads(qs[j], 0), hot[b], bias[j]))
            dps.append(nt(keys[:, HD:], both_heads(qs[j], 2 * HD)))
        for (j, _), s, dp in zip(pairs, ss, dps):
            update(j, s, dp)

    for a in range(HALF):
        keys = runs_of(k_own, k_other, range(a + 1))
        blocks = hot[: a + 1].reshape((a + 1) * RUN, CH)
        js = (a, a + HALF)
        ss = [scores(keys[:, :HD], both_heads(qs[j], 0), blocks, bias[j]) for j in js]
        dps = [nt(keys[:, HD:], both_heads(qs[j], 2 * HD)) for j in js]
        for j, s, dp in zip(js, ss, dps):
            update(j, s, dp)

    for_rest(mm, body)
    t = total[...]
    some = t > 0.0
    safe = jnp.where(some, t, 1.0)
    out_ref[:, 0:1, :] = jnp.where(some, top[...] * FACTOR + jnp.log2(safe), LOW)
    out_ref[:, 1:2, :] = dot[...] / safe


def grad_kernel(ids, mm, hot, bias, k_own, k_other, *refs):
    st_ref, qs, dq_ref, own_ref, other_ref, lse, delta, dq_acc, dkv_acc = refs
    parts = st_ref[:, :, 0:1, :]
    high = jnp.max(parts, axis=0)
    shares = jnp.exp2(parts - high[None])
    sums = jnp.sum(shares, axis=0)
    lse[...] = high + jnp.log2(sums)
    delta[...] = jnp.sum(shares * st_ref[:, :, 1:2, :], axis=0) / sums
    dkv_acc[HALF:] = jnp.zeros((HALF, RUN, 2 * HD), f32)

    def start(j, keys, blocks):
        q2 = both_heads(qs[j], 0)
        o2 = both_heads(qs[j], 2 * HD)
        s = scores(keys[:, :HD], q2, blocks, bias[j])
        dp = nt(keys[:, HD:], o2)
        p = jnp.exp2(s * FACTOR - lse[j])
        ds = (p * (dp - delta[j]) * SCALE).astype(bf16)
        return q2, o2, ds, p.astype(bf16)

    def query_grad(ds, keys):
        return lax.dot_general(
            ds, keys[:, :HD], (((0,), (0,)), ((), ())), preferred_element_type=f32
        )

    def visit(js, keys, blocks):
        parts = [start(j, keys, blocks) for j in js]
        q2, o2 = (jnp.concatenate([t[n] for t in parts], axis=0) for n in (0, 1))
        ds, p = (jnp.concatenate([t[n] for t in parts], axis=1) for n in (2, 3))
        return query_grad(ds, keys), nn(ds, q2), nn(p, o2)

    def body(pairs):
        keys = [runs_of(k_own, k_other, [b]) for _, b in pairs]
        parts = [start(j, k, hot[b]) for (j, b), k in zip(pairs, keys)]
        for (j, b), k, (q2, o2, ds, p) in zip(pairs, keys, parts):
            dq_acc[j] += query_grad(ds, k)
            dkv_acc[b, :, :HD] += nn(ds, q2)
            dkv_acc[b, :, HD:] += nn(p, o2)

    for a in reversed(range(HALF)):
        runs = a + 1
        keys = runs_of(k_own, k_other, range(runs))
        blocks = hot[:runs].reshape(runs * RUN, CH)
        dq, dk, dv = visit((a, a + HALF), keys, blocks)
        dq_acc[a] = dq[: 2 * CH]
        dq_acc[a + HALF] = dq[2 * CH :]
        dk, dv = dk.reshape(runs, RUN, HD), dv.reshape(runs, RUN, HD)
        if runs == HALF:
            dkv_acc[:runs, :, :HD] = dk
            dkv_acc[:runs, :, HD:] = dv
        else:
            dkv_acc[:runs, :, :HD] += dk
            dkv_acc[:runs, :, HD:] += dv

    for_rest(mm, body)
    for j in range(NZ):
        t = dq_acc[j]
        dq_ref[j] = jnp.concatenate([t[:CH], t[CH:]], axis=1).astype(bf16)
    for slot in range(NRUN):
        for xh in range(NXH):
            y, x = slot // NXL, xh * NXL + slot % NXL
            for n, ref in enumerate((own_ref, other_ref)):
                at = (n * NXH + xh) * CH
                ref[y, x] = dkv_acc[slot, at : at + CH, :].astype(bf16)


SMEM = pl.BlockSpec(memory_space=pltpu.SMEM)
VMEM = pl.BlockSpec(memory_space=pltpu.VMEM)
DATA = VMEM
BIG = 44 << 20
QUERIES = jax.ShapeDtypeStruct((NZ, CH, 4 * HD), bf16)
MASKS = (
    jax.ShapeDtypeStruct((NRUN, RUN, CH), bf16),
    jax.ShapeDtypeStruct((NZ, CH, CH), bf16),
)
ROW = pltpu.VMEM((NZ, 1, 2 * CH), f32)


def per_device(queries, key_states, value_states, grad_output, block_ids):
    z, xh, core = (lax.axis_index(n) for n in ROWS)
    y, xl = (lax.axis_index(n) for n in COLS)
    qo, kv = pl.pallas_call(
        pack_kernel,
        out_shape=(
            jax.ShapeDtypeStruct((CH, 4 * HD), bf16),
            jax.ShapeDtypeStruct((NY * NX, CH, 2 * HD), bf16),
        ),
        in_specs=[VMEM] * 4,
        out_specs=(VMEM, VMEM),
    )(queries, grad_output, key_states, value_states)

    def swap(t):
        return lax.ppermute(t, "core", [(0, 1), (1, 0)])

    k_own = lax.all_to_all(kv, ("y",) + XAX, 0, 0)
    pieces = {0: qo}
    for s in range(1, NZ // 2 + 1):
        pieces[s] = shift(pieces[s - 1], "z", NZ, 1)
        if s < NZ // 2:
            pieces[-s] = shift(pieces[1 - s], "z", NZ, -1)
    q_pieces = [pieces[s] for s in Q_SHIFTS]
    k_late, _, _ = lax.optimization_barrier((k_own, pieces[-3], pieces[3]))
    k_other = swap(k_late)

    qid = block_ids.reshape(HALF, NXH * NCORE * NY * NXL, CH)
    place = ((xh * NCORE + core) * NY + y) * NXL + xl
    qid = lax.dynamic_slice_in_dim(qid, place, 1, 1)
    kid = block_ids.reshape(HALF, NZ, RUN)
    kid = lax.dynamic_slice_in_dim(kid, z, 1, 1).reshape(HALF, RUN)
    mm = jnp.stack([qid[:, 0, 0], qid[:, 0, CH - 1], kid[:, 0], kid[:, RUN - 1]])
    kid = kid.reshape(HALF, NXH, NCORE, CH)
    kid = jnp.where(core == 0, kid, kid[:, :, ::-1]).swapaxes(1, 2).reshape(HALF, RUN)
    ids = jnp.stack([z, y, xh, xl, core]).astype(i32)
    stats, queries, hot, bias = stats_call((ids, mm, qid, kid, k_own, k_other), q_pieces)
    keys = (ids, mm, hot, bias, k_own, k_other)
    stats = jnp.broadcast_to(stats[None], (NZ,) + stats.shape)
    stats = lax.all_to_all(stats, "z", 0, 0)
    dq, own, other = grad_call(keys, stats, queries)

    dq = lax.all_to_all(dq, "z", 0, 0)
    pair = (own.astype(f32) + swap(other).astype(f32)).astype(bf16)
    pair = scatter(pair, y, "y", NY)
    pair = scatter(pair, xh * NXL + xl, XAX, NX)
    dq = jnp.sum(dq.astype(f32), axis=0).astype(bf16)
    return dq, pair[:, :HD], pair[:, HD:]


def scatter(t, me, axis, size):
    def part(k):
        return lax.dynamic_index_in_dim(t, (me + k) % size, 0, keepdims=False)

    got = [part(0)] + [shift(part(k), axis, size, k) for k in range(1, size)]
    return sum(g.astype(f32) for g in got).astype(bf16)


KEY_SPECS = [SMEM, SMEM] + [VMEM] * 4


def stats_call(keys, q_pieces):
    return pl.pallas_call(
        stats_kernel,
        out_shape=(jax.ShapeDtypeStruct((NZ, 2, 2 * CH), f32), QUERIES) + MASKS,
        in_specs=KEY_SPECS + [VMEM] * NZ,
        out_specs=(VMEM,) * 4,
        scratch_shapes=[ROW, ROW, ROW],
        compiler_params=pltpu.CompilerParams(vmem_limit_bytes=BIG),
    )(*keys, *q_pieces)


def grad_call(keys, stats, queries):
    return pl.pallas_call(
        grad_kernel,
        out_shape=(
            jax.ShapeDtypeStruct((NZ, CH, 2 * HD), bf16),
            jax.ShapeDtypeStruct((NY, NX, CH, 2 * HD), bf16),
            jax.ShapeDtypeStruct((NY, NX, CH, 2 * HD), bf16),
        ),
        in_specs=KEY_SPECS + [VMEM] * 2,
        out_specs=(VMEM,) * 3,
        scratch_shapes=[
            ROW,
            ROW,
            pltpu.VMEM((NZ, 2 * CH, HD), f32),
            pltpu.VMEM((NRUN, RUN, 2 * HD), f32),
        ],
        compiler_params=pltpu.CompilerParams(vmem_limit_bytes=BIG),
    )(*keys, stats, queries)


def solution(mesh):
    fine = Mesh(mesh.devices.reshape(NZ, NXH, NCORE, NY, NXL), ROWS + COLS)
    by_row = P(ROWS + COLS, None)
    by_col = P(COLS + ROWS, None)
    return jax.shard_map(
        per_device,
        mesh=fine,
        in_specs=(by_row, by_col, by_col, by_row, P()),
        out_specs=(by_row, by_col, by_col),
        check_vma=False,
    )
```

```python
import functools
import math

import jax
import jax.numpy as jnp
from jax import lax
from jax.experimental import pallas as pl
from jax.experimental.pallas import tpu as pltpu
from jax.sharding import Mesh
from jax.sharding import PartitionSpec as P

bf16 = jnp.bfloat16
f32 = jnp.float32
i32 = jnp.int32
NZ, NXH, NCORE, NY, NXL = 8, 2, 2, 4, 2
NX = NXH * NXL
CH = 128
HD = 128
RUN = NXH * NCORE * CH
NRUN = NY * NXL
HALF = NRUN // 2
NBLK = 32
LOW = -1e30
SCALE = 1.0 / math.sqrt(HD)
FACTOR = SCALE * math.log2(math.e)
ROWS = ("z", "xh", "core")
COLS = ("y", "xl")
XAX = ("xh", "xl")


def shift(x, axis, size, by):
    return lax.ppermute(x, axis, [(i, (i + by) % size) for i in range(size)])


def nt(a, b):
    return lax.dot_general(a, b, (((1,), (1,)), ((), ())), preferred_element_type=f32)


def nn(a, b):
    return lax.dot_general(a, b, (((1,), (0,)), ((), ())), preferred_element_type=f32)


def load_queries(ids, q_pieces, qs):
    for by, piece in zip(Q_SHIFTS, q_pieces):
        qs[(ids[0] - by) % NZ] = piece[...]


def run_of(own_ref, other_ref, slot):
    at = slot // NXL * NX + slot % NXL
    return [ref[at + xh * NXL] for ref in (own_ref, other_ref) for xh in range(NXH)]


def runs_of(own_ref, other_ref, slots):
    return jnp.concatenate([t for n in slots for t in run_of(own_ref, other_ref, n)], axis=0)


Q_SHIFTS = (0, 1, -1, 2, -2, 3, -3, 4)


def pack_kernel(q_ref, o_ref, k_ref, v_ref, qo_ref, kv_ref):
    qo_ref[:, : 2 * HD] = q_ref[...]
    qo_ref[:, 2 * HD :] = o_ref[...]
    for i in range(NY * NX):
        kv_ref[i, :, :HD] = k_ref[...]
        kv_ref[i, :, HD:] = v_ref[...]


def make_masks(qid_ref, kid_ref, hot, bias):
    lane = lax.broadcasted_iota(i32, (RUN, CH), 1)
    for b in range(HALF):
        col = jnp.broadcast_to(kid_ref[b : b + 1, :], (CH, RUN)).T
        hot[b] = jnp.where(lane == col, 1.0, 0.0).astype(bf16)
        hot[b + HALF] = jnp.where(lane == col + NBLK, 1.0, 0.0).astype(bf16)
    lane = lax.broadcasted_iota(i32, (CH, CH), 1)
    for a in range(HALF):
        col = jnp.broadcast_to(qid_ref[a], (CH, CH)).T
        bias[a] = jnp.where(lane <= col, 0.0, LOW).astype(bf16)
        seen = (lane < col) | (lane == col + NBLK)
        bias[a + HALF] = jnp.where(seen, 0.0, LOW).astype(bf16)


def both_heads(qo, base):
    return jnp.concatenate([qo[:, base : base + HD], qo[:, base + HD : base + 2 * HD]], axis=0)


def scores(k, q2, hot, bias):
    return nt(
        jnp.concatenate([k, hot], axis=1),
        jnp.concatenate([q2, jnp.concatenate([bias, bias], axis=0)], axis=1),
    )


def for_rest(mm, body):
    def shared(a, b):
        return (mm[2, b] <= mm[1, a]) & (mm[3, b] >= mm[0, a])

    def any_of(flags):
        return functools.reduce(jnp.logical_or, flags)

    steps = range(HALF - 1)

    @pl.when(any_of([shared(a, a) for a in range(HALF)]))
    def _():
        body([(a + HALF, a + HALF) for a in range(HALF)])

    @pl.when(any_of([shared(a, a + 1) for a in steps]))
    def _():
        body([(a, a + 1) for a in steps] + [(a + HALF, a + HALF + 1) for a in steps])

    @pl.when(any_of([shared(a + 1, a) for a in steps]))
    def _():
        body([(a + HALF + 1, a + HALF) for a in steps])


def stats_kernel(ids, mm, qid_ref, kid_ref, k_own, k_other, *refs):
    q_pieces, (out_ref, qs, hot, bias, top, total, dot) = refs[:NZ], refs[NZ:]
    load_queries(ids, q_pieces, qs)
    make_masks(qid_ref, kid_ref, hot, bias)
    top[...] = jnp.full(top.shape, LOW, f32)
    total[...] = jnp.zeros(total.shape, f32)
    dot[...] = jnp.zeros(dot.shape, f32)

    def update(j, s, dp):
        old = top[j]
        new = jnp.maximum(old, jnp.max(s, axis=0, keepdims=True))
        p = jnp.exp2((s - new) * FACTOR)
        f = jnp.exp2((old - new) * FACTOR)
        top[j] = new
        total[j] = total[j] * f + jnp.sum(p, axis=0, keepdims=True)
        dot[j] = dot[j] * f + jnp.sum(p * dp, axis=0, keepdims=True)

    def body(pairs):
        ss, dps = [], []
        for j, b in pairs:
            keys = runs_of(k_own, k_other, [b])
            ss.append(scores(keys[:, :HD], both_heads(qs[j], 0), hot[b], bias[j]))
            dps.append(nt(keys[:, HD:], both_heads(qs[j], 2 * HD)))
        for (j, _), s, dp in zip(pairs, ss, dps):
            update(j, s, dp)

    for a in range(HALF):
        keys = runs_of(k_own, k_other, range(a + 1))
        blocks = hot[: a + 1].reshape((a + 1) * RUN, CH)
        js = (a, a + HALF)
        ss = [scores(keys[:, :HD], both_heads(qs[j], 0), blocks, bias[j]) for j in js]
        dps = [nt(keys[:, HD:], both_heads(qs[j], 2 * HD)) for j in js]
        for j, s, dp in zip(js, ss, dps):
            update(j, s, dp)

    for_rest(mm, body)
    t = total[...]
    some = t > 0.0
    safe = jnp.where(some, t, 1.0)
    out_ref[:, 0:1, :] = jnp.where(some, top[...] * FACTOR + jnp.log2(safe), LOW)
    out_ref[:, 1:2, :] = dot[...] / safe


def grad_kernel(ids, mm, hot, bias, k_own, k_other, *refs):
    st_ref, qs, other_ref, own_ref, dq_ref, lse, delta, dq_acc, dkv_acc = refs
    parts = st_ref[:, :, 0:1, :]
    high = jnp.max(parts, axis=0)
    shares = jnp.exp2(parts - high[None])
    sums = jnp.sum(shares, axis=0)
    lse[...] = high + jnp.log2(sums)
    delta[...] = jnp.sum(shares * st_ref[:, :, 1:2, :], axis=0) / sums
    dkv_acc[HALF:] = jnp.zeros((HALF, RUN, 2 * HD), f32)

    def start(j, keys, blocks):
        q2 = both_heads(qs[j], 0)
        o2 = both_heads(qs[j], 2 * HD)
        s = scores(keys[:, :HD], q2, blocks, bias[j])
        dp = nt(keys[:, HD:], o2)
        p = jnp.exp2(s * FACTOR - lse[j])
        ds = (p * (dp - delta[j]) * SCALE).astype(bf16)
        return q2, o2, ds, p.astype(bf16)

    def query_grad(ds, keys):
        return lax.dot_general(
            ds, keys[:, :HD], (((0,), (0,)), ((), ())), preferred_element_type=f32
        )

    def visit(js, keys, blocks):
        parts = [start(j, keys, blocks) for j in js]
        q2, o2 = (jnp.concatenate([t[n] for t in parts], axis=0) for n in (0, 1))
        ds, p = (jnp.concatenate([t[n] for t in parts], axis=1) for n in (2, 3))
        return query_grad(ds, keys), nn(ds, q2), nn(p, o2)

    def body(pairs):
        keys = [runs_of(k_own, k_other, [b]) for _, b in pairs]
        parts = [start(j, k, hot[b]) for (j, b), k in zip(pairs, keys)]
        for (j, b), k, (q2, o2, ds, p) in zip(pairs, keys, parts):
            dq_acc[j] += query_grad(ds, k)
            dkv_acc[b, :, :HD] += nn(ds, q2)
            dkv_acc[b, :, HD:] += nn(p, o2)

    for a in reversed(range(HALF)):
        runs = a + 1
        keys = runs_of(k_own, k_other, range(runs))
        blocks = hot[:runs].reshape(runs * RUN, CH)
        dq, dk, dv = visit((a, a + HALF), keys, blocks)
        dq_acc[a] = dq[: 2 * CH]
        dq_acc[a + HALF] = dq[2 * CH :]
        dk, dv = dk.reshape(runs, RUN, HD), dv.reshape(runs, RUN, HD)
        if runs == HALF:
            dkv_acc[:runs, :, :HD] = dk
            dkv_acc[:runs, :, HD:] = dv
        else:
            dkv_acc[:runs, :, :HD] += dk
            dkv_acc[:runs, :, HD:] += dv

    for_rest(mm, body)
    for j in range(NZ):
        t = dq_acc[j]
        dq_ref[j] = jnp.concatenate([t[:CH], t[CH:]], axis=1).astype(bf16)
    for slot in range(NRUN):
        for xh in range(NXH):
            y, x = slot // NXL, xh * NXL + slot % NXL
            for n, ref in enumerate((own_ref, other_ref)):
                at = (n * NXH + xh) * CH
                ref[y, x] = dkv_acc[slot, at : at + CH, :].astype(bf16)


def add_kernel(ids, own_ref, other_ref, *outs):
    for k, out in enumerate(outs):
        at = (ids[1] + k) % NY
        out[...] = (own_ref[at].astype(f32) + other_ref[at].astype(f32)).astype(bf16)


SMEM = pl.BlockSpec(memory_space=pltpu.SMEM)
VMEM = pl.BlockSpec(memory_space=pltpu.VMEM)
DATA = VMEM
BIG = 44 << 20
QUERIES = jax.ShapeDtypeStruct((NZ, CH, 4 * HD), bf16)
MASKS = (
    jax.ShapeDtypeStruct((NRUN, RUN, CH), bf16),
    jax.ShapeDtypeStruct((NZ, CH, CH), bf16),
)
ROW = pltpu.VMEM((NZ, 1, 2 * CH), f32)


def per_device(queries, key_states, value_states, grad_output, block_ids):
    z, xh, core = (lax.axis_index(n) for n in ROWS)
    y, xl = (lax.axis_index(n) for n in COLS)
    qo, kv = pl.pallas_call(
        pack_kernel,
        out_shape=(
            jax.ShapeDtypeStruct((CH, 4 * HD), bf16),
            jax.ShapeDtypeStruct((NY * NX, CH, 2 * HD), bf16),
        ),
        in_specs=[VMEM] * 4,
        out_specs=(VMEM, VMEM),
    )(queries, grad_output, key_states, value_states)

    def swap(t):
        return lax.ppermute(t, "core", [(0, 1), (1, 0)])

    k_own = lax.all_to_all(kv, ("y",) + XAX, 0, 0)
    pieces = {0: qo}
    for s in range(1, NZ // 2 + 1):
        pieces[s] = shift(pieces[s - 1], "z", NZ, 1)
        if s < NZ // 2:
            pieces[-s] = shift(pieces[1 - s], "z", NZ, -1)
    q_pieces = [pieces[s] for s in Q_SHIFTS]
    k_late, _, _ = lax.optimization_barrier((k_own, pieces[-3], pieces[3]))
    k_other = swap(k_late)

    qid = block_ids.reshape(HALF, NXH * NCORE * NY * NXL, CH)
    place = ((xh * NCORE + core) * NY + y) * NXL + xl
    qid = lax.dynamic_slice_in_dim(qid, place, 1, 1)
    kid = block_ids.reshape(HALF, NZ, RUN)
    kid = lax.dynamic_slice_in_dim(kid, z, 1, 1).reshape(HALF, RUN)
    mm = jnp.stack([qid[:, 0, 0], qid[:, 0, CH - 1], kid[:, 0], kid[:, RUN - 1]])
    kid = kid.reshape(HALF, NXH, NCORE, CH)
    kid = jnp.where(core == 0, kid, kid[:, :, ::-1]).swapaxes(1, 2).reshape(HALF, RUN)
    ids = jnp.stack([z, y, xh, xl, core]).astype(i32)
    stats, queries, hot, bias = stats_call((ids, mm, qid, kid, k_own, k_other), q_pieces)
    keys = (ids, mm, hot, bias, k_own, k_other)
    stats = jnp.broadcast_to(stats[None], (NZ,) + stats.shape)
    stats = lax.all_to_all(stats, "z", 0, 0)
    other, own, dq = grad_call(keys, stats, queries)

    dq = lax.all_to_all(dq, "z", 0, 0)
    parts = add_call(ids, own, swap(other))
    got = [parts[0]] + [shift(t, "y", NY, k) for k, t in enumerate(parts) if k]
    pair = sum(g.astype(f32) for g in got).astype(bf16)
    pair = scatter(pair, xh * NXL + xl, XAX, NX)
    dq = jnp.sum(dq.astype(f32), axis=0).astype(bf16)
    return dq, pair[:, :HD], pair[:, HD:]


def scatter(t, me, axis, size):
    def part(k):
        return lax.dynamic_index_in_dim(t, (me + k) % size, 0, keepdims=False)

    got = [part(0)] + [shift(part(k), axis, size, k) for k in range(1, size)]
    return sum(g.astype(f32) for g in got).astype(bf16)


KEY_SPECS = [SMEM, SMEM] + [VMEM] * 4


def stats_call(keys, q_pieces):
    return pl.pallas_call(
        stats_kernel,
        out_shape=(jax.ShapeDtypeStruct((NZ, 2, 2 * CH), f32), QUERIES) + MASKS,
        in_specs=KEY_SPECS + [VMEM] * NZ,
        out_specs=(VMEM,) * 4,
        scratch_shapes=[ROW, ROW, ROW],
        compiler_params=pltpu.CompilerParams(vmem_limit_bytes=BIG),
    )(*keys, *q_pieces)


def grad_call(keys, stats, queries):
    return pl.pallas_call(
        grad_kernel,
        out_shape=(
            jax.ShapeDtypeStruct((NY, NX, CH, 2 * HD), bf16),
            jax.ShapeDtypeStruct((NY, NX, CH, 2 * HD), bf16),
            jax.ShapeDtypeStruct((NZ, CH, 2 * HD), bf16),
        ),
        in_specs=KEY_SPECS + [VMEM] * 2,
        out_specs=(VMEM,) * 3,
        scratch_shapes=[
            ROW,
            ROW,
            pltpu.VMEM((NZ, 2 * CH, HD), f32),
            pltpu.VMEM((NRUN, RUN, 2 * HD), f32),
        ],
        compiler_params=pltpu.CompilerParams(vmem_limit_bytes=BIG),
    )(*keys, stats, queries)


def add_call(ids, own, other):
    return pl.pallas_call(
        add_kernel,
        out_shape=[jax.ShapeDtypeStruct((NX, CH, 2 * HD), bf16)] * NY,
        in_specs=[SMEM] + [VMEM] * 2,
        out_specs=[VMEM] * NY,
        compiler_params=pltpu.CompilerParams(vmem_limit_bytes=BIG),
    )(ids, own, other)


def solution(mesh):
    fine = Mesh(mesh.devices.reshape(NZ, NXH, NCORE, NY, NXL), ROWS + COLS)
    by_row = P(ROWS + COLS, None)
    by_col = P(COLS + ROWS, None)
    return jax.shard_map(
        per_device,
        mesh=fine,
        in_specs=(by_row, by_col, by_col, by_row, P()),
        out_specs=(by_row, by_col, by_col),
        check_vma=False,
    )
```
